32 devices in a mesh: ctx: 16 (over z, x, core), ch: 2 (over y).
Axes of the slice: x: 2, y: 2, z: 4, core: 2. Of those that a mesh axis runs over, the one named last changes fastest.
Arguments:
- hidden: bfloat16 [4096, 2048], P('ctx', 'ch'), may hold values from -6 to 6
- channel_perm: int32 [2048], replicated, may hold values from 0 to 2047, each once
- input_weight: bfloat16 [2048, 2048], P(None, 'ch'), may hold values from -0.125 to 0.125
- state_weight: bfloat16 [2048, 32], replicated, may hold values from -0.03125 to 0.03125
- step_weight: bfloat16 [2048, 32], P(None, 'ch'), may hold values from -0.25 to 0.25
- step_bias: float32 [32], P('ch'), may hold values from -5 to -1
- decay_log: float32 [32], P('ch'), may hold values from -6 to 2
- filter_taps: float32 [4, 2048], P(None, 'ch'), may hold values from -3 to 3
- skip_gain: float32 [2048], P('ch'), may hold values from 0.5 to 1.5
- output_weight: bfloat16 [2048, 2048], P('ch'), may hold values from -0.125 to 0.125
- cotangent: bfloat16 [4096, 2048], P('ctx', 'ch'), may hold values from -0.119628906 to 0.119628906
Outputs:
- layer_out: bfloat16 [4096, 2048], P('ctx', 'ch')
- grad_input_weight: float32 [2048, 2048], P(None, 'ch')
- grad_filter: float32 [4, 2048], P(None, 'ch')
- grad_skip: float32 [2048], P('ch')
The draws below stay inside these ranges and needn't reach their ends.
Inputs may be any that keep to these rules, and one draw needn't show every extreme that they name: channel_perm holds each channel number once.
All inputs are finite; a program needn't handle non-finite values.
Results may differ from the reference program's by a relative error of at most 0.012.
Values may be sent and summed in bfloat16 or wider, within the bound.
A program may use at most 128 MiB of HBM per device.

```python
import jax
import jax.numpy as jnp
from jax import lax

D = 2048
STATE = 16
CONV = 4
BLOCK = 256
HEADS = 32
SEQ = 4096


def level_of(key, shape, cuts, smallest, largest):
    def one(axis_at, shards_of):
        steps = jax.random.uniform(jax.random.fold_in(jax.random.fold_in(key, 6), axis_at), (shards_of,), jnp.float32, smallest / len(cuts), largest / len(cuts))
        return jnp.repeat(jnp.exp(steps), shape[axis_at] // shards_of).reshape((-1,) + (1,) * (len(shape) - axis_at - 1))

    level = one(*cuts[0])
    for cut in cuts[1:]:
        level = level * one(*cut)
    return level


def normal_values(own_key, shape, scale, reach, split=(), kind=jnp.bfloat16):
    factor_of = level_of(own_key, shape, split, -0.22, 0.18) if split else 1.0
    array = jax.random.normal(own_key, shape, jnp.float32) * scale * factor_of
    return jnp.minimum(jnp.maximum(array, -reach), reach).astype(kind)


def setup_inputs(seed: int = 0) -> dict:
    streams_of = jax.random.split(jax.random.key(seed), 12)
    return {
        "hidden": normal_values(streams_of[0], (SEQ, D), 1.0, 6.0, ((0, 16), (1, 2))),
        "channel_perm": jax.random.permutation(streams_of[1], D).astype(jnp.int32),
        "input_weight": normal_values(streams_of[2], (D, D), D ** -0.5, 0.125, ((1, 2),)),
        "state_weight": normal_values(streams_of[3], (D, 2 * STATE), (16 * D) ** -0.5, 0.03125),
        "step_weight": normal_values(streams_of[4], (D, HEADS), (D // 4) ** -0.5, 0.25, ((1, 2),)),
        "step_bias": jnp.clip(-5.0 + 4.0 * jax.random.uniform(streams_of[5], (HEADS,), jnp.float32) ** level_of(streams_of[5], (HEADS,), ((0, 2),), -0.2, 0.2), -5.0, -1.0),
        "decay_log": jnp.clip(-6.0 + 8.0 * jax.random.uniform(streams_of[6], (HEADS,), jnp.float32) ** level_of(streams_of[6], (HEADS,), ((0, 2),), -0.2, 0.2), -6.0, 2.0),
        "filter_taps": normal_values(streams_of[7], (CONV, D), 0.5, 3.0, ((1, 2),), jnp.float32),
        "skip_gain": jnp.clip(0.5 + 1.0 * jax.random.uniform(streams_of[8], (D,), jnp.float32) ** level_of(streams_of[8], (D,), ((0, 2),), -0.2, 0.2), 0.5, 1.5),
        "output_weight": normal_values(streams_of[9], (D, D), D ** -0.5, 0.125, ((0, 2),)),
        "cotangent": normal_values(streams_of[10], (SEQ, D), 0.02, 0.119628906, ((0, 16), (1, 2))),
    }


exact_mode = lax.Precision.HIGHEST


def conv_apply(padded, taps):
    width = taps.shape[0] - 1
    length = padded.shape[0] - width
    total = jnp.zeros((length, padded.shape[1]), jnp.float32)
    for tap_index in range(width + 1):
        total = total + taps[tap_index][None, :] * padded[width - tap_index:width - tap_index + length]
    return total


def conv_back(extended, taps):
    width = taps.shape[0] - 1
    length = extended.shape[0] - width
    total = jnp.zeros((length, extended.shape[1]), jnp.float32)
    for tap_index in range(width + 1):
        total = total + taps[tap_index][None, :] * extended[tap_index:tap_index + length]
    return total


def tap_grads(slope, padded):
    width = padded.shape[0] - slope.shape[0]
    length = slope.shape[0]
    return jnp.stack([jnp.sum(slope * padded[width - tap_index:width - tap_index + length], axis=0) for tap_index in range(width + 1)])


def silu_slope(values):
    sigma = jax.nn.sigmoid(values)
    return sigma * (1.0 + values * (1.0 - sigma))


def per_head(values, sizes):
    length, width = values.shape
    heads = sizes.shape[1]
    return (values.reshape(length, heads, width // heads) * sizes[:, :, None]).reshape(length, width)


def branch_inputs(embedded, padded, state_weight, step_weight, step_bias, decay_log, filter_taps):
    projected = jnp.dot(embedded, state_weight, preferred_element_type=jnp.float32)
    states = projected.shape[1] // 2
    writes = projected[:, :states]
    reads = projected[:, states:]
    sizes = jax.nn.softplus(jnp.dot(embedded, step_weight, preferred_element_type=jnp.float32) + step_bias[None, :])
    decays = -jnp.exp(decay_log)[None, :] * sizes
    before = conv_apply(padded, filter_taps)
    return writes, reads, sizes, decays, before, jax.nn.silu(before)


def causal_scan(inputs, step_size, log_decay, write_vec, read_vec):
    length, width = inputs.shape
    heads = step_size.shape[1]
    depth = width // heads
    states = write_vec.shape[1]
    blocks = length // BLOCK
    lower_mask = jnp.arange(BLOCK)[:, None] >= jnp.arange(BLOCK)[None, :]

    def advance(carried, portion):
        values, sizes, decays, writes, reads = portion
        running = jnp.cumsum(decays, axis=0)
        source = values.reshape(BLOCK, heads, depth) * sizes[:, :, None]
        scores = jnp.dot(reads, writes.T, precision=exact_mode)
        spread = running.T[:, :, None] - running.T[:, None, :]
        weights = jnp.where(lower_mask[None], jnp.exp(jnp.where(lower_mask[None], spread, 0.0)), 0.0) * scores[None]
        result = jnp.einsum("hts,shp->thp", weights, source, precision=exact_mode)
        result = result + jnp.exp(running)[:, :, None] * jnp.einsum("tn,hpn->thp", reads, carried, precision=exact_mode)
        remain = jnp.exp(running[-1][None, :] - running)
        carried = jnp.exp(running[-1])[:, None, None] * carried + jnp.einsum("shp,sn->hpn", source * remain[:, :, None], writes, precision=exact_mode)
        return carried, result.reshape(BLOCK, width)

    portions = (inputs.reshape(blocks, BLOCK, width), step_size.reshape(blocks, BLOCK, heads), log_decay.reshape(blocks, BLOCK, heads), write_vec.reshape(blocks, BLOCK, states), read_vec.reshape(blocks, BLOCK, states))
    start = jnp.zeros((heads, depth, states), jnp.float32)
    final, outputs = lax.scan(advance, start, portions)
    return outputs.reshape(length, width), final


def anti_scan(grads, log_decay, write_vec, read_vec):
    length, width = grads.shape
    heads = log_decay.shape[1]
    depth = width // heads
    states = write_vec.shape[1]
    blocks = length // BLOCK
    upper_mask = jnp.arange(BLOCK)[None, :] >= jnp.arange(BLOCK)[:, None]

    def retreat(carried, portion):
        values, decays, writes, reads = portion
        running = jnp.cumsum(decays, axis=0)
        source = values.reshape(BLOCK, heads, depth)
        scores = jnp.dot(writes, reads.T, precision=exact_mode)
        spread = running.T[:, None, :] - running.T[:, :, None]
        weights = jnp.where(upper_mask[None], jnp.exp(jnp.where(upper_mask[None], spread, 0.0)), 0.0) * scores[None]
        result = jnp.einsum("hts,shp->thp", weights, source, precision=exact_mode)
        remain = jnp.exp(running[-1][None, :] - running)
        result = result + remain[:, :, None] * jnp.einsum("tn,hpn->thp", writes, carried, precision=exact_mode)
        carried = jnp.exp(running[-1])[:, None, None] * carried + jnp.einsum("shp,sn->hpn", source * jnp.exp(running)[:, :, None], reads, precision=exact_mode)
        return carried, result.reshape(BLOCK, width)

    portions = (grads.reshape(blocks, BLOCK, width), log_decay.reshape(blocks, BLOCK, heads), write_vec.reshape(blocks, BLOCK, states), read_vec.reshape(blocks, BLOCK, states))
    start = jnp.zeros((heads, depth, states), jnp.float32)
    final, outputs = lax.scan(retreat, start, portions, reverse=True)
    return outputs.reshape(length, width), final


def reference(hidden, channel_perm, input_weight, state_weight, step_weight, step_bias, decay_log, filter_taps, skip_gain, output_weight, cotangent):
    width = CONV - 1
    fwd_embed = hidden
    rev_embed = jnp.flip(jnp.take(hidden, channel_perm, axis=1), 0)
    branches = []
    for embedded in (fwd_embed, rev_embed):
        inner = jnp.dot(embedded, input_weight, preferred_element_type=jnp.float32).astype(jnp.bfloat16)
        padded = jnp.concatenate([jnp.zeros((width, inner.shape[1]), jnp.float32), inner.astype(jnp.float32)], 0)
        writes, reads, sizes, decays, before, activated = branch_inputs(embedded, padded, state_weight, step_weight, step_bias, decay_log, filter_taps)
        scanned, final = causal_scan(activated, sizes, decays, writes, reads)
        branches.append((embedded, padded, writes, reads, sizes, decays, before, activated, scanned))
    fwd_part, rev_part = branches
    mixed_sum = (fwd_part[8] + jnp.flip(rev_part[8], 0) + skip_gain[None, :] * (fwd_part[7] + jnp.flip(rev_part[7], 0))).astype(jnp.bfloat16)
    layer_out = jnp.dot(mixed_sum, output_weight, preferred_element_type=jnp.float32).astype(jnp.bfloat16)
    back = jnp.dot(cotangent, output_weight.T, preferred_element_type=jnp.float32)
    grad_input_weight = jnp.zeros(input_weight.shape, jnp.float32)
    grad_filter = jnp.zeros(filter_taps.shape, jnp.float32)
    for branch_back, part in ((back, fwd_part), (jnp.flip(back, 0), rev_part)):
        embedded, padded, writes, reads, sizes, decays, before, activated, scanned = part
        adjoint, final = anti_scan(branch_back, decays, writes, reads)
        grad_act = skip_gain[None, :] * branch_back + per_head(adjoint, sizes)
        slope = grad_act * silu_slope(before)
        extended = jnp.concatenate([slope, jnp.zeros((width, slope.shape[1]), jnp.float32)], 0)
        grad_inner = conv_back(extended, filter_taps).astype(jnp.bfloat16)
        grad_input_weight = grad_input_weight + jnp.dot(embedded.T, grad_inner, preferred_element_type=jnp.float32)
        grad_filter = grad_filter + tap_grads(slope, padded)
    grad_skip = jnp.sum(back * (fwd_part[7] + jnp.flip(rev_part[7], 0)), axis=0)
    return (layer_out, grad_input_weight, grad_filter, grad_skip)
```

```python
import functools

import jax
import jax.numpy as jnp
from jax import lax
from jax.experimental import pallas as pl
from jax.experimental.pallas import tpu as pltpu
from jax.sharding import PartitionSpec as P

EXACT = lax.Precision.HIGHEST
F32, BF16 = jnp.float32, jnp.bfloat16
RIM = 16


def dot(a, b, dims=((1,), (0,)), precision=None):
    return lax.dot_general(
        a, b, (dims, ((), ())), preferred_element_type=F32, precision=precision
    )


def shifted(x, taps_at, branch, length):
    start = RIM - taps_at if branch == 0 else taps_at
    return x[start : start + length]


def head_lanes(per_head_col, first, group, depth, length):
    lane = lax.broadcasted_iota(jnp.int32, (length, group * depth), 1)
    value = jnp.broadcast_to(per_head_col[:, first : first + 1], lane.shape)
    for extra in range(1, group):
        value = jnp.where(
            lane >= extra * depth,
            jnp.broadcast_to(per_head_col[:, first + extra : first + extra + 1], lane.shape),
            value,
        )
    return value


def local_kernel(
    depth, group, xf, xr, back, sizes, run, run_t, writes, reads, taps, gain,
    mixed, base, slopes, states, skip,
):
    length, width = back.shape
    row = lax.broadcasted_iota(jnp.int32, (length, length), 0)
    col = lax.broadcasted_iota(jnp.int32, (length, length), 1)
    scores = []
    for b in range(2):
        full = dot(reads[b], writes[b], ((1,), (1,)), EXACT)
        scores.append(jnp.where(row >= col if b == 0 else row <= col, full, 0.0))
    span = group * depth
    lane = lax.broadcasted_iota(jnp.int32, (length, span), 1)
    for q in range(width // span):
        cols = slice(q * span, (q + 1) * span)
        grad = back[:, cols]
        grad16 = grad.astype(BF16)
        total = None
        acts = None
        for b in range(2):
            x = (xf, xr)[b][:, cols].astype(F32)
            before = sum(
                taps[k : k + 1, cols] * shifted(x, k, b, length) for k in range(taps.shape[0])
            )
            sigma = jax.nn.sigmoid(before)
            act = before * sigma
            slope = sigma * (1.0 + before * (1.0 - sigma))
            size = head_lanes(sizes[b], q * group, group, depth, length)
            source = act * size
            source16 = source.astype(BF16)
            scan = adjoint = None
            for g in range(group):
                h = q * group + g
                spread = run[b, :, h : h + 1] - run_t[b, h : h + 1, :]
                decay = (jnp.exp(jnp.minimum(spread, 0.0)) * scores[b]).astype(BF16)
                one = dot(decay, source16)
                two = dot(decay, grad16, ((0,), (0,)))
                scan = one if g == 0 else jnp.where(lane >= g * depth, one, scan)
                adjoint = two if g == 0 else jnp.where(lane >= g * depth, two, adjoint)
            running = head_lanes(run[b], q * group, group, depth, length)
            end = running[length - 1 :] if b == 0 else running[:1]
            remain = jnp.exp(end - running)
            states[b, :, cols] = dot(
                writes[b].astype(BF16), (source * remain).astype(BF16), ((0,), (0,))
            ).astype(BF16)
            states[2 + b, :, cols] = dot(
                reads[b].astype(BF16), (grad * jnp.exp(running)).astype(BF16), ((0,), (0,))
            ).astype(BF16)
            base[b, :, cols] = (gain[:, cols] * grad + size * adjoint) * slope
            slopes[b, :, cols] = slope * size * remain
            total = scan if b == 0 else total + scan
            acts = act if b == 0 else acts + act
        mixed[:, cols] = total + gain[:, cols] * acts
        skip[:, cols] = jnp.sum(grad * acts, axis=0, keepdims=True)


def carry_kernel(
    depth, group, xf, xr, mixed_in, base, slopes, run, writes, reads, carried, taps,
    mixed, inner, edge, slope_edge, filt,
):
    length, width = mixed_in.shape
    span = group * depth
    taken = taps.shape[0]
    zeros = jnp.zeros((8, span), F32)
    for q in range(width // span):
        cols = slice(q * span, (q + 1) * span)
        total = mixed_in[:, cols]
        grads = [0.0] * taken
        for b in range(2):
            running = head_lanes(run[b], q * group, group, depth, length)
            total = total + jnp.exp(running) * dot(
                reads[b].astype(BF16), carried[b, :, cols].astype(BF16)
            )
            slope = base[b, :, cols] + slopes[b, :, cols] * dot(
                writes[b].astype(BF16), carried[2 + b, :, cols].astype(BF16)
            )
            x = (xf, xr)[b][:, cols].astype(F32)
            for k in range(taken):
                grads[k] = grads[k] + jnp.sum(
                    slope * shifted(x, k, b, length), axis=0, keepdims=True
                )
            if b == 0:
                longer = jnp.concatenate([slope, zeros], axis=0)
                parts = [longer[k : k + length] for k in range(taken)]
                slope_edge[b, :, cols] = slope[:8]
            else:
                longer = jnp.concatenate([zeros, slope], axis=0)
                parts = [longer[8 - k : 8 - k + length] for k in range(taken)]
                slope_edge[b, :, cols] = slope[length - 8 :]
            grad = sum(taps[k : k + 1, cols] * parts[k] for k in range(taken))
            inner[b * length : (b + 1) * length, cols] = grad.astype(BF16)
            edge[b, :, cols] = grad[length - 8 :] if b == 0 else grad[:8]
        mixed[:, cols] = total.astype(BF16)
        for k in range(taken):
            filt[k : k + 1, cols] = grads[k]


def vmem_call(body, shapes, *operands):
    spec = pl.BlockSpec(memory_space=pltpu.VMEM)
    return pl.pallas_call(
        body,
        out_shape=[jax.ShapeDtypeStruct(*s) for s in shapes],
        in_specs=[spec] * len(operands),
        out_specs=[spec] * len(shapes),
        compiler_params=pltpu.CompilerParams(vmem_limit_bytes=48 * 1024 * 1024),
    )(*operands)


def per_device(
    hidden, channel_perm, input_weight, state_weight, step_weight, step_bias, decay_log,
    filter_taps, skip_gain, output_weight, cotangent,
):
    length = hidden.shape[0]
    taken, width = filter_taps.shape
    heads = step_weight.shape[1]
    depth = width // heads
    group = max(1, 128 // depth)
    states = state_weight.shape[1] // 2
    model = input_weight.shape[0]
    count, me = lax.axis_size("ctx"), lax.axis_index("ctx")
    pair = lax.axis_size("ch") == 2
    side = lax.axis_index("ch")
    up = [(i, i + 1) for i in range(count - 1)]
    down = [(i + 1, i) for i in range(count - 1)]
    swap = [(0, 1), (1, 0)]

    def gathered(part):
        if not pair:
            return lax.all_gather(part, "ch", axis=1, tiled=True)
        other = lax.ppermute(part, "ch", swap)
        return jnp.where(
            side == 0,
            jnp.concatenate([part, other], 1),
            jnp.concatenate([other, part], 1),
        )

    embed = gathered(hidden)
    upstream = gathered(cotangent)
    onehot = (
        lax.broadcasted_iota(jnp.int32, (model, model), 0) == channel_perm[None, :]
    ).astype(BF16)
    both = jnp.concatenate([embed, dot(embed, onehot).astype(BF16)], 0)
    inner = dot(both, input_weight).astype(BF16)
    small = dot(both, jnp.concatenate([state_weight, step_weight], 1)).reshape(2, length, -1)
    fwd_rim = lax.ppermute(inner[length - RIM : length], "ctx", up)
    rev_rim = lax.ppermute(inner[length : length + RIM], "ctx", down)
    writes = small[:, :, :states]
    reads = small[:, :, states : 2 * states]
    sizes = jax.nn.softplus(small[:, :, 2 * states :] + step_bias[None, None, :])
    decays = -jnp.exp(decay_log)[None, None, :] * sizes
    totals = lax.all_gather(jnp.sum(decays, axis=1), "ctx")
    lower = jnp.tril(jnp.ones((length, length), F32))
    sums = jnp.stack([lower, lower.T])
    run = jnp.einsum("bts,bsh->bth", sums, decays, precision=EXACT)
    run_t = jnp.swapaxes(run, 1, 2)
    back = dot(upstream, output_weight, ((1,), (1,)))
    xf = jnp.concatenate([fwd_rim, inner[:length]], 0)
    xr = jnp.concatenate([inner[length:], rev_rim], 0)
    full = (length, width)
    mixed, base, slopes, ends, skip = vmem_call(
        functools.partial(local_kernel, depth, group),
        [
            (full, F32),
            ((2,) + full, F32),
            ((2,) + full, F32),
            ((4, states, width), BF16),
            ((1, width), F32),
        ],
        xf, xr, back, sizes, run, run_t, writes, reads, filter_taps, skip_gain[None, :],
    )
    pieces = lax.all_gather(ends, "ctx")
    j = jnp.arange(count)
    between = ((j[:, None] < j[None, :]) & (j[None, :] < me)) | (
        (j[None, :] < j[:, None]) & (j[None, :] > me)
    )
    weight = jnp.exp(jnp.einsum("ji,ibh->jbh", between.astype(F32), totals, precision=EXACT))
    earlier = jnp.where((j < me)[:, None], 1.0, 0.0)
    later = jnp.where((j > me)[:, None], 1.0, 0.0)
    kinds = jnp.stack(
        [
            weight[:, 0] * earlier,
            weight[:, 1] * later,
            weight[:, 0] * later,
            weight[:, 1] * earlier,
        ],
        axis=1,
    )
    kinds = jnp.repeat(kinds, depth, axis=2)
    carried = jnp.sum(kinds[:, :, None, :] * pieces.astype(F32), axis=0)
    mixed16, partial_grad, edge, slope_edge, filt = vmem_call(
        functools.partial(carry_kernel, depth, group),
        [
            (full, BF16),
            ((2 * length, width), BF16),
            ((2, 8, width), F32),
            ((2, 8, width), F32),
            ((taken, width), F32),
        ],
        xf, xr, mixed, base, slopes, run, writes, reads, carried, filter_taps,
    )
    fwd_after = lax.ppermute(slope_edge[0], "ctx", down)
    rev_after = lax.ppermute(slope_edge[1], "ctx", up)
    if pair:
        half = output_weight.shape[1] // 2
        theirs = lax.dynamic_slice_in_dim(output_weight, (1 - side) * half, half, 1)
        mine = lax.dynamic_slice_in_dim(output_weight, side * half, half, 1)
        arrived = lax.ppermute(dot(mixed16, theirs).astype(BF16), "ch", swap)
        layer_out = (dot(mixed16, mine) + arrived.astype(F32)).astype(BF16)
    else:
        layer_out = lax.psum_scatter(
            dot(mixed16, output_weight), "ch", scatter_dimension=1, tiled=True
        ).astype(BF16)
    zeros = jnp.zeros((8, width), F32)
    ahead = jnp.concatenate([zeros, fwd_after], 0)
    behind = jnp.concatenate([rev_after, zeros], 0)
    fwd_edge = edge[0] + sum(filter_taps[k][None] * ahead[k : k + 8] for k in range(taken))
    rev_edge = edge[1] + sum(
        filter_taps[k][None] * behind[8 - k : 16 - k] for k in range(taken)
    )
    grad_inner = jnp.concatenate(
        [
            partial_grad[: length - 8],
            fwd_edge.astype(BF16),
            rev_edge.astype(BF16),
            partial_grad[length + 8 :],
        ],
        0,
    )
    weight_local = dot(both, grad_inner, ((0,), (0,))).astype(BF16)
    tiny = lax.psum(jnp.concatenate([filt, skip], 0), "ctx")
    weight_sum = lax.psum_scatter(weight_local, "ctx", scatter_dimension=0, tiled=True)
    weight_grad = lax.all_gather(weight_sum, "ctx", axis=0, tiled=True).astype(F32)
    return (layer_out, weight_grad, tiny[:taken], tiny[taken])


def solution(mesh):
    placed = (
        P("ctx", "ch"), P(), P(None, "ch"), P(), P(None, "ch"), P("ch"), P("ch"),
        P(None, "ch"), P("ch"), P("ch", None), P("ctx", "ch"),
    )
    return jax.shard_map(
        per_device,
        mesh=mesh,
        in_specs=placed,
        out_specs=(P("ctx", "ch"), P(None, "ch"), P(None, "ch"), P("ch")),
        check_vma=False,
    )
```

```python
import functools

import jax
import jax.numpy as jnp
from jax import lax
from jax.experimental import pallas as pl
from jax.experimental.pallas import tpu as pltpu
from jax.sharding import PartitionSpec as P

EXACT = lax.Precision.HIGHEST
F32, BF16 = jnp.float32, jnp.bfloat16
RIM = 16


def dot(a, b, dims=((1,), (0,)), precision=None):
    return lax.dot_general(
        a, b, (dims, ((), ())), preferred_element_type=F32, precision=precision
    )


def shifted(x, taps_at, branch, length):
    start = RIM - taps_at if branch == 0 else taps_at
    return x[start : start + length]


def head_lanes(per_head_col, first, group, depth, length):
    lane = lax.broadcasted_iota(jnp.int32, (length, group * depth), 1)
    value = jnp.broadcast_to(per_head_col[:, first : first + 1], lane.shape)
    for extra in range(1, group):
        value = jnp.where(
            lane >= extra * depth,
            jnp.broadcast_to(per_head_col[:, first + extra : first + extra + 1], lane.shape),
            value,
        )
    return value


def local_kernel(
    depth, group, xf, xr, back, sizes, run, run_t, writes, reads, taps, gain,
    mixed, base, slopes, states, skip,
):
    length, width = back.shape
    row = lax.broadcasted_iota(jnp.int32, (length, length), 0)
    col = lax.broadcasted_iota(jnp.int32, (length, length), 1)
    scores = []
    for b in range(2):
        full = dot(reads[b], writes[b], ((1,), (1,)), EXACT)
        scores.append(jnp.where(row >= col if b == 0 else row <= col, full, 0.0))
    span = group * depth
    lane = lax.broadcasted_iota(jnp.int32, (length, span), 1)
    for q in range(width // span):
        cols = slice(q * span, (q + 1) * span)
        grad = back[:, cols]
        grad16 = grad.astype(BF16)
        total = None
        acts = None
        for b in range(2):
            x = (xf, xr)[b][:, cols].astype(F32)
            before = sum(
                taps[k : k + 1, cols] * shifted(x, k, b, length) for k in range(taps.shape[0])
            )
            sigma = jax.nn.sigmoid(before)
            act = before * sigma
            slope = sigma * (1.0 + before * (1.0 - sigma))
            size = head_lanes(sizes[b], q * group, group, depth, length)
            source = act * size
            source16 = source.astype(BF16)
            scan = adjoint = None
            for g in range(group):
                h = q * group + g
                spread = run[b, :, h : h + 1] - run_t[b, h : h + 1, :]
                decay = (jnp.exp(jnp.minimum(spread, 0.0)) * scores[b]).astype(BF16)
                one = dot(decay, source16)
                two = dot(decay, grad16, ((0,), (0,)))
                scan = one if g == 0 else jnp.where(lane >= g * depth, one, scan)
                adjoint = two if g == 0 else jnp.where(lane >= g * depth, two, adjoint)
            running = head_lanes(run[b], q * group, group, depth, length)
            end = running[length - 1 :] if b == 0 else running[:1]
            remain = jnp.exp(end - running)
            states[b, :, cols] = dot(
                writes[b].astype(BF16), (source * remain).astype(BF16), ((0,), (0,))
            ).astype(BF16)
            states[2 + b, :, cols] = dot(
                reads[b].astype(BF16), (grad * jnp.exp(running)).astype(BF16), ((0,), (0,))
            ).astype(BF16)
            base[b, :, cols] = (gain[:, cols] * grad + size * adjoint) * slope
            slopes[b, :, cols] = slope * size * remain
            total = scan if b == 0 else total + scan
            acts = act if b == 0 else acts + act
        mixed[:, cols] = total + gain[:, cols] * acts
        skip[:, cols] = jnp.sum(grad * acts, axis=0, keepdims=True)


def carry_kernel(
    depth, group, xf, xr, mixed_in, base, slopes, run, writes, reads, carried, taps,
    mixed, inner, edge, slope_edge, filt,
):
    length, width = mixed_in.shape
    span = group * depth
    taken = taps.shape[0]
    zeros = jnp.zeros((8, span), F32)
    for q in range(width // span):
        cols = slice(q * span, (q + 1) * span)
        total = mixed_in[:, cols]
        grads = [0.0] * taken
        for b in range(2):
            running = head_lanes(run[b], q * group, group, depth, length)
            total = total + jnp.exp(running) * dot(
                reads[b].astype(BF16), carried[b, :, cols].astype(BF16)
            )
            slope = base[b, :, cols] + slopes[b, :, cols] * dot(
                writes[b].astype(BF16), carried[2 + b, :, cols].astype(BF16)
            )
            x = (xf, xr)[b][:, cols].astype(F32)
            for k in range(taken):
                grads[k] = grads[k] + jnp.sum(
                    slope * shifted(x, k, b, length), axis=0, keepdims=True
                )
            if b == 0:
                longer = jnp.concatenate([slope, zeros], axis=0)
                parts = [longer[k : k + length] for k in range(taken)]
                slope_edge[b, :, cols] = slope[:8]
            else:
                longer = jnp.concatenate([zeros, slope], axis=0)
                parts = [longer[8 - k : 8 - k + length] for k in range(taken)]
                slope_edge[b, :, cols] = slope[length - 8 :]
            grad = sum(taps[k : k + 1, cols] * parts[k] for k in range(taken))
            inner[b * length : (b + 1) * length, cols] = grad.astype(BF16)
            edge[b, :, cols] = grad[length - 8 :] if b == 0 else grad[:8]
        mixed[:, cols] = total.astype(BF16)
        for k in range(taken):
            filt[k : k + 1, cols] = grads[k]


def three_parts(value):
    parts = []
    for _ in range(3):
        top = lax.reduce_precision(value, 8, 7)
        parts.append(top.astype(BF16))
        value = value - top
    rows = jnp.concatenate(parts, 0)
    return jnp.pad(rows, ((0, -rows.shape[0] % 16), (0, 0)))


def summed_rows(value, axis):
    count, me = lax.axis_size(axis), lax.axis_index(axis)
    bits = [1 << b for b in range(count.bit_length() - 1)]
    orders = (bits, bits[:1] + bits[2:] + bits[1:2])
    half = value.shape[0] // 2
    parts = [value[:half], value[half:]]

    def swapped(part, bit):
        return lax.ppermute(part, axis, [(i, i ^ bit) for i in range(count)])

    for step in range(len(bits)):
        for p in range(2):
            bit = orders[p][step]
            upper = (me // bit) % 2
            rows = parts[p].shape[0] // 2
            keep = lax.dynamic_slice_in_dim(parts[p], upper * rows, rows, 0)
            send = lax.dynamic_slice_in_dim(parts[p], (1 - upper) * rows, rows, 0)
            parts[p] = (keep.astype(F32) + swapped(send, bit).astype(F32)).astype(BF16)
    for step in reversed(range(len(bits))):
        for p in range(2):
            bit = orders[p][step]
            upper = (me // bit) % 2
            other = swapped(parts[p], bit)
            parts[p] = jnp.where(
                upper == 0,
                jnp.concatenate([parts[p], other], 0),
                jnp.concatenate([other, parts[p]], 0),
            )
    return jnp.concatenate(parts, 0)


def vmem_call(body, shapes, *operands):
    spec = pl.BlockSpec(memory_space=pltpu.VMEM)
    return pl.pallas_call(
        body,
        out_shape=[jax.ShapeDtypeStruct(*s) for s in shapes],
        in_specs=[spec] * len(operands),
        out_specs=[spec] * len(shapes),
        compiler_params=pltpu.CompilerParams(vmem_limit_bytes=48 * 1024 * 1024),
    )(*operands)


def per_device(
    hidden, channel_perm, input_weight, state_weight, step_weight, step_bias, decay_log,
    filter_taps, skip_gain, output_weight, cotangent,
):
    length = hidden.shape[0]
    taken, width = filter_taps.shape
    heads = step_weight.shape[1]
    depth = width // heads
    group = max(1, 128 // depth)
    states = state_weight.shape[1] // 2
    model = input_weight.shape[0]
    count, me = lax.axis_size("ctx"), lax.axis_index("ctx")
    pair = lax.axis_size("ch") == 2
    side = lax.axis_index("ch")
    up = [(i, i + 1) for i in range(count - 1)]
    down = [(i + 1, i) for i in range(count - 1)]
    swap = [(0, 1), (1, 0)]

    def gathered(part):
        if not pair:
            return lax.all_gather(part, "ch", axis=1, tiled=True)
        other = lax.ppermute(part, "ch", swap)
        return jnp.where(
            side == 0,
            jnp.concatenate([part, other], 1),
            jnp.concatenate([other, part], 1),
        )

    embed = gathered(hidden)
    upstream = gathered(cotangent)
    onehot = (
        lax.broadcasted_iota(jnp.int32, (model, model), 0) == channel_perm[None, :]
    ).astype(BF16)
    both = jnp.concatenate([embed, dot(embed, onehot).astype(BF16)], 0)
    inner = dot(both, input_weight).astype(BF16)
    small = dot(both, jnp.concatenate([state_weight, step_weight], 1)).reshape(2, length, -1)
    fwd_rim = lax.ppermute(inner[length - RIM : length], "ctx", up)
    rev_rim = lax.ppermute(inner[length : length + RIM], "ctx", down)
    writes = small[:, :, :states]
    reads = small[:, :, states : 2 * states]
    sizes = jax.nn.softplus(small[:, :, 2 * states :] + step_bias[None, None, :])
    decays = -jnp.exp(decay_log)[None, None, :] * sizes
    totals = three_parts(jnp.repeat(jnp.sum(decays, axis=1), depth, axis=1))
    lower = jnp.tril(jnp.ones((length, length), F32))
    sums = jnp.stack([lower, lower.T])
    run = jnp.einsum("bts,bsh->bth", sums, decays, precision=EXACT)
    run_t = jnp.swapaxes(run, 1, 2)
    back = dot(upstream, output_weight, ((1,), (1,)))
    xf = jnp.concatenate([fwd_rim, inner[:length]], 0)
    xr = jnp.concatenate([inner[length:], rev_rim], 0)
    full = (length, width)
    mixed, base, slopes, ends, skip = vmem_call(
        functools.partial(local_kernel, depth, group),
        [
            (full, F32),
            ((2,) + full, F32),
            ((2,) + full, F32),
            ((4, states, width), BF16),
            ((1, width), F32),
        ],
        xf, xr, back, sizes, run, run_t, writes, reads, filter_taps, skip_gain[None, :],
    )
    rows = 4 * states
    packed = jnp.concatenate([ends.reshape(rows, width), totals], 0)
    arrived = lax.all_gather(packed, "ctx")
    pieces = arrived[:, :rows].reshape(count, 4, states, width)
    totals = arrived[:, rows : rows + 6].astype(F32).reshape(count, 3, 2, heads, depth)
    totals = jnp.sum(totals[..., 0], axis=1)
    j = jnp.arange(count)
    between = ((j[:, None] < j[None, :]) & (j[None, :] < me)) | (
        (j[None, :] < j[:, None]) & (j[None, :] > me)
    )
    weight = jnp.exp(jnp.einsum("ji,ibh->jbh", between.astype(F32), totals, precision=EXACT))
    earlier = jnp.where((j < me)[:, None], 1.0, 0.0)
    later = jnp.where((j > me)[:, None], 1.0, 0.0)
    kinds = jnp.stack(
        [
            weight[:, 0] * earlier,
            weight[:, 1] * later,
            weight[:, 0] * later,
            weight[:, 1] * earlier,
        ],
        axis=1,
    )
    kinds = jnp.repeat(kinds, depth, axis=2)
    carried = jnp.sum(kinds[:, :, None, :] * pieces.astype(F32), axis=0)
    mixed16, partial_grad, edge, slope_edge, filt = vmem_call(
        functools.partial(carry_kernel, depth, group),
        [
            (full, BF16),
            ((2 * length, width), BF16),
            ((2, 8, width), F32),
            ((2, 8, width), F32),
            ((taken, width), F32),
        ],
        xf, xr, mixed, base, slopes, run, writes, reads, carried, filter_taps,
    )
    fwd_after = lax.ppermute(slope_edge[0], "ctx", down)
    rev_after = lax.ppermute(slope_edge[1], "ctx", up)
    if pair:
        half = output_weight.shape[1] // 2
        theirs = lax.dynamic_slice_in_dim(output_weight, (1 - side) * half, half, 1)
        mine = lax.dynamic_slice_in_dim(output_weight, side * half, half, 1)
        arrived = lax.ppermute(dot(mixed16, theirs).astype(BF16), "ch", swap)
        layer_out = (dot(mixed16, mine) + arrived.astype(F32)).astype(BF16)
    else:
        layer_out = lax.psum_scatter(
            dot(mixed16, output_weight), "ch", scatter_dimension=1, tiled=True
        ).astype(BF16)
    zeros = jnp.zeros((8, width), F32)
    ahead = jnp.concatenate([zeros, fwd_after], 0)
    behind = jnp.concatenate([rev_after, zeros], 0)
    fwd_edge = edge[0] + sum(filter_taps[k][None] * ahead[k : k + 8] for k in range(taken))
    rev_edge = edge[1] + sum(
        filter_taps[k][None] * behind[8 - k : 16 - k] for k in range(taken)
    )
    grad_inner = jnp.concatenate(
        [
            partial_grad[: length - 8],
            fwd_edge.astype(BF16),
            rev_edge.astype(BF16),
            partial_grad[length + 8 :],
        ],
        0,
    )
    weight_local = dot(both, grad_inner, ((0,), (0,))).astype(BF16)
    tiny = lax.psum(jnp.concatenate([filt, skip], 0), "ctx")
    weight_grad = summed_rows(weight_local, "ctx").astype(F32)
    return (layer_out, weight_grad, tiny[:taken], tiny[taken])


def solution(mesh):
    placed = (
        P("ctx", "ch"), P(), P(None, "ch"), P(), P(None, "ch"), P("ch"), P("ch"),
        P(None, "ch"), P("ch"), P("ch", None), P("ctx", "ch"),
    )
    return jax.shard_map(
        per_device,
        mesh=mesh,
        in_specs=placed,
        out_specs=(P("ctx", "ch"), P(None, "ch"), P(None, "ch"), P("ch")),
        check_vma=False,
    )
```

```python
import functools

import jax
import jax.numpy as jnp
from jax import lax
from jax.experimental import pallas as pl
from jax.experimental.pallas import tpu as pltpu
from jax.sharding import PartitionSpec as P

EXACT = lax.Precision.HIGHEST
F32, BF16 = jnp.float32, jnp.bfloat16
RIM = 16


def dot(a, b, dims=((1,), (0,)), precision=None):
    return lax.dot_general(
        a, b, (dims, ((), ())), preferred_element_type=F32, precision=precision
    )


def shifted(x, taps_at, branch, length):
    start = RIM - taps_at if branch == 0 else taps_at
    return x[start : start + length]


def head_lanes(per_head_col, first, group, depth, length):
    lane = lax.broadcasted_iota(jnp.int32, (length, group * depth), 1)
    value = jnp.broadcast_to(per_head_col[:, first : first + 1], lane.shape)
    for extra in range(1, group):
        value = jnp.where(
            lane >= extra * depth,
            jnp.broadcast_to(per_head_col[:, first + extra : first + extra + 1], lane.shape),
            value,
        )
    return value


def local_kernel(
    depth, group, xf, xr, back, sizes, run, run_t, writes, reads, taps, gain,
    mixed, base, slopes, states, skip,
):
    length, width = back.shape
    row = lax.broadcasted_iota(jnp.int32, (length, length), 0)
    col = lax.broadcasted_iota(jnp.int32, (length, length), 1)
    scores = []
    for b in range(2):
        full = dot(reads[b], writes[b], ((1,), (1,)), EXACT)
        scores.append(jnp.where(row >= col if b == 0 else row <= col, full, 0.0))
    span = group * depth
    lane = lax.broadcasted_iota(jnp.int32, (length, span), 1)
    for q in range(width // span):
        cols = slice(q * span, (q + 1) * span)
        grad = back[:, cols]
        grad16 = grad.astype(BF16)
        total = None
        acts = None
        for b in range(2):
            x = (xf, xr)[b][:, cols].astype(F32)
            before = sum(
                taps[k : k + 1, cols] * shifted(x, k, b, length) for k in range(taps.shape[0])
            )
            sigma = jax.nn.sigmoid(before)
            act = before * sigma
            slope = sigma * (1.0 + before * (1.0 - sigma))
            size = head_lanes(sizes[b], q * group, group, depth, length)
            source = act * size
            source16 = source.astype(BF16)
            scan = adjoint = None
            for g in range(group):
                h = q * group + g
                spread = run[b, :, h : h + 1] - run_t[b, h : h + 1, :]
                decay = (jnp.exp(jnp.minimum(spread, 0.0)) * scores[b]).astype(BF16)
                one = dot(decay, source16)
                two = dot(decay, grad16, ((0,), (0,)))
                scan = one if g == 0 else jnp.where(lane >= g * depth, one, scan)
                adjoint = two if g == 0 else jnp.where(lane >= g * depth, two, adjoint)
            running = head_lanes(run[b], q * group, group, depth, length)
            end = running[length - 1 :] if b == 0 else running[:1]
            remain = jnp.exp(end - running)
            states[b, :, cols] = dot(
                writes[b].astype(BF16), (source * remain).astype(BF16), ((0,), (0,))
            ).astype(BF16)
            states[2 + b, :, cols] = dot(
                reads[b].astype(BF16), (grad * jnp.exp(running)).astype(BF16), ((0,), (0,))
            ).astype(BF16)
            base[b, :, cols] = (gain[:, cols] * grad + size * adjoint) * slope
            slopes[b, :, cols] = slope * size * remain
            total = scan if b == 0 else total + scan
            acts = act if b == 0 else acts + act
        mixed[:, cols] = total + gain[:, cols] * acts
        skip[:, cols] = jnp.sum(grad * acts, axis=0, keepdims=True)


def carry_kernel(
    depth, group, xf, xr, mixed_in, base, slopes, run, writes, reads, carried, taps,
    mixed, inner, edge, slope_edge, filt,
):
    length, width = mixed_in.shape
    span = group * depth
    taken = taps.shape[0]
    zeros = jnp.zeros((8, span), F32)
    for q in range(width // span):
        cols = slice(q * span, (q + 1) * span)
        total = mixed_in[:, cols]
        grads = [0.0] * taken
        for b in range(2):
            running = head_lanes(run[b], q * group, group, depth, length)
            total = total + jnp.exp(running) * dot(
                reads[b].astype(BF16), carried[b, :, cols].astype(BF16)
            )
            slope = base[b, :, cols] + slopes[b, :, cols] * dot(
                writes[b].astype(BF16), carried[2 + b, :, cols].astype(BF16)
            )
            x = (xf, xr)[b][:, cols].astype(F32)
            for k in range(taken):
                grads[k] = grads[k] + jnp.sum(
                    slope * shifted(x, k, b, length), axis=0, keepdims=True
                )
            if b == 0:
                longer = jnp.concatenate([slope, zeros], axis=0)
                parts = [longer[k : k + length] for k in range(taken)]
                slope_edge[b, :, cols] = slope[:8]
            else:
                longer = jnp.concatenate([zeros, slope], axis=0)
                parts = [longer[8 - k : 8 - k + length] for k in range(taken)]
                slope_edge[b, :, cols] = slope[length - 8 :]
            grad = sum(taps[k : k + 1, cols] * parts[k] for k in range(taken))
            inner[b * length : (b + 1) * length, cols] = grad.astype(BF16)
            edge[b, :, cols] = grad[length - 8 :] if b == 0 else grad[:8]
        mixed[:, cols] = total.astype(BF16)
        for k in range(taken):
            filt[k : k + 1, cols] = grads[k]


def three_parts(value):
    parts = []
    for _ in range(3):
        top = lax.reduce_precision(value, 8, 7)
        parts.append(top.astype(BF16))
        value = value - top
    rows = jnp.concatenate(parts, 0)
    return jnp.pad(rows, ((0, -rows.shape[0] % 16), (0, 0)))


def summed_whole(value, axis):
    count = lax.axis_size(axis)
    for b in range(count.bit_length() - 1):
        value = value + lax.ppermute(value, axis, [(i, i ^ (1 << b)) for i in range(count)])
    return value


def entering(ends, totals, axis):
    count, me = lax.axis_size(axis), lax.axis_index(axis)
    kinds, states, width = ends.shape
    rows = kinds * states
    group = ends.astype(F32)
    result = jnp.zeros_like(group)
    passed = jnp.zeros((kinds, width), F32)
    forward = jnp.array([True, False, False, True])
    for b in range(count.bit_length() - 1):
        bit = 1 << b
        packed = jnp.concatenate(
            [group.astype(BF16).reshape(rows, width), three_parts(totals)], 0
        )
        arrived = lax.ppermute(packed, axis, [(i, i ^ bit) for i in range(count)]).astype(F32)
        other = arrived[:rows].reshape(kinds, states, width)
        added = sum(arrived[rows + 2 * k : rows + 2 * k + 2] for k in range(3))
        source = (forward == ((me // bit) % 2 == 1))[:, None]
        theirs, ours = jnp.tile(added, (2, 1)), jnp.tile(totals, (2, 1))
        result = result + jnp.where(source, jnp.exp(passed), 0.0)[:, None] * other
        passed = passed + jnp.where(source, theirs, 0.0)
        group = (
            jnp.where(source, jnp.exp(ours), 1.0)[:, None] * other
            + jnp.where(source, 1.0, jnp.exp(theirs))[:, None] * group
        )
        totals = totals + added
    return result


def summed_rows(value, axis):
    count, me = lax.axis_size(axis), lax.axis_index(axis)
    bits = [1 << b for b in range(count.bit_length() - 1)]
    orders = (bits, bits[:1] + bits[2:] + bits[1:2])
    half = value.shape[0] // 2
    parts = [value[:half], value[half:]]

    def swapped(part, bit):
        return lax.ppermute(part, axis, [(i, i ^ bit) for i in range(count)])

    for step in range(len(bits)):
        for p in range(2):
            bit = orders[p][step]
            upper = (me // bit) % 2
            rows = parts[p].shape[0] // 2
            keep = lax.dynamic_slice_in_dim(parts[p], upper * rows, rows, 0)
            send = lax.dynamic_slice_in_dim(parts[p], (1 - upper) * rows, rows, 0)
            parts[p] = (keep.astype(F32) + swapped(send, bit).astype(F32)).astype(BF16)
    for step in reversed(range(len(bits))):
        for p in range(2):
            bit = orders[p][step]
            upper = (me // bit) % 2
            other = swapped(parts[p], bit)
            parts[p] = jnp.where(
                upper == 0,
                jnp.concatenate([parts[p], other], 0),
                jnp.concatenate([other, parts[p]], 0),
            )
    return jnp.concatenate(parts, 0)


def vmem_call(body, shapes, *operands):
    spec = pl.BlockSpec(memory_space=pltpu.VMEM)
    return pl.pallas_call(
        body,
        out_shape=[jax.ShapeDtypeStruct(*s) for s in shapes],
        in_specs=[spec] * len(operands),
        out_specs=[spec] * len(shapes),
        compiler_params=pltpu.CompilerParams(vmem_limit_bytes=48 * 1024 * 1024),
    )(*operands)


def per_device(
    hidden, channel_perm, input_weight, state_weight, step_weight, step_bias, decay_log,
    filter_taps, skip_gain, output_weight, cotangent,
):
    length = hidden.shape[0]
    taken, width = filter_taps.shape
    heads = step_weight.shape[1]
    depth = width // heads
    group = max(1, 128 // depth)
    states = state_weight.shape[1] // 2
    model = input_weight.shape[0]
    count, me = lax.axis_size("ctx"), lax.axis_index("ctx")
    pair = lax.axis_size("ch") == 2
    side = lax.axis_index("ch")
    up = [(i, i + 1) for i in range(count - 1)]
    down = [(i + 1, i) for i in range(count - 1)]
    swap = [(0, 1), (1, 0)]

    def gathered(part):
        if not pair:
            return lax.all_gather(part, "ch", axis=1, tiled=True)
        other = lax.ppermute(part, "ch", swap)
        return jnp.where(
            side == 0,
            jnp.concatenate([part, other], 1),
            jnp.concatenate([other, part], 1),
        )

    embed = gathered(hidden)
    upstream = gathered(cotangent)
    onehot = (
        lax.broadcasted_iota(jnp.int32, (model, model), 0) == channel_perm[None, :]
    ).astype(BF16)
    both = jnp.concatenate([embed, dot(embed, onehot).astype(BF16)], 0)
    inner = dot(both, input_weight).astype(BF16)
    small = dot(both, jnp.concatenate([state_weight, step_weight], 1)).reshape(2, length, -1)
    fwd_rim = lax.ppermute(inner[length - RIM : length], "ctx", up)
    rev_rim = lax.ppermute(inner[length : length + RIM], "ctx", down)
    writes = small[:, :, :states]
    reads = small[:, :, states : 2 * states]
    sizes = jax.nn.softplus(small[:, :, 2 * states :] + step_bias[None, None, :])
    decays = -jnp.exp(decay_log)[None, None, :] * sizes
    totals = jnp.repeat(jnp.sum(decays, axis=1), depth, axis=1)
    lower = jnp.tril(jnp.ones((length, length), F32))
    sums = jnp.stack([lower, lower.T])
    run = jnp.einsum("bts,bsh->bth", sums, decays, precision=EXACT)
    run_t = jnp.swapaxes(run, 1, 2)
    back = dot(upstream, output_weight, ((1,), (1,)))
    xf = jnp.concatenate([fwd_rim, inner[:length]], 0)
    xr = jnp.concatenate([inner[length:], rev_rim], 0)
    full = (length, width)
    mixed, base, slopes, ends, skip = vmem_call(
        functools.partial(local_kernel, depth, group),
        [
            (full, F32),
            ((2,) + full, F32),
            ((2,) + full, F32),
            ((4, states, width), BF16),
            ((1, width), F32),
        ],
        xf, xr, back, sizes, run, run_t, writes, reads, filter_taps, skip_gain[None, :],
    )
    carried = entering(ends, totals, "ctx")
    mixed16, partial_grad, edge, slope_edge, filt = vmem_call(
        functools.partial(carry_kernel, depth, group),
        [
            (full, BF16),
            ((2 * length, width), BF16),
            ((2, 8, width), F32),
            ((2, 8, width), F32),
            ((taken, width), F32),
        ],
        xf, xr, mixed, base, slopes, run, writes, reads, carried, filter_taps,
    )
    fwd_after = lax.ppermute(slope_edge[0], "ctx", down)
    rev_after = lax.ppermute(slope_edge[1], "ctx", up)
    if pair:
        half = output_weight.shape[1] // 2
        theirs = lax.dynamic_slice_in_dim(output_weight, (1 - side) * half, half, 1)
        mine = lax.dynamic_slice_in_dim(output_weight, side * half, half, 1)
        arrived = lax.ppermute(dot(mixed16, theirs).astype(BF16), "ch", swap)
        layer_out = (dot(mixed16, mine) + arrived.astype(F32)).astype(BF16)
    else:
        layer_out = lax.psum_scatter(
            dot(mixed16, output_weight), "ch", scatter_dimension=1, tiled=True
        ).astype(BF16)
    zeros = jnp.zeros((8, width), F32)
    ahead = jnp.concatenate([zeros, fwd_after], 0)
    behind = jnp.concatenate([rev_after, zeros], 0)
    fwd_edge = edge[0] + sum(filter_taps[k][None] * ahead[k : k + 8] for k in range(taken))
    rev_edge = edge[1] + sum(
        filter_taps[k][None] * behind[8 - k : 16 - k] for k in range(taken)
    )
    grad_inner = jnp.concatenate(
        [
            partial_grad[: length - 8],
            fwd_edge.astype(BF16),
            rev_edge.astype(BF16),
            partial_grad[length + 8 :],
        ],
        0,
    )
    weight_local = dot(both, grad_inner, ((0,), (0,))).astype(BF16)
    tiny = summed_whole(jnp.concatenate([filt, skip], 0), "ctx")
    weight_grad = summed_rows(weight_local, "ctx").astype(F32)
    return (layer_out, weight_grad, tiny[:taken], tiny[taken])


def solution(mesh):
    placed = (
        P("ctx", "ch"), P(), P(None, "ch"), P(), P(None, "ch"), P("ch"), P("ch"),
        P(None, "ch"), P("ch"), P("ch", None), P("ctx", "ch"),
    )
    return jax.shard_map(
        per_device,
        mesh=mesh,
        in_specs=placed,
        out_specs=(P("ctx", "ch"), P(None, "ch"), P(None, "ch"), P("ch")),
        check_vma=False,
    )
```

```python
import functools

import jax
import jax.numpy as jnp
from jax import lax
from jax.experimental import pallas as pl
from jax.experimental.pallas import tpu as pltpu
from jax.sharding import PartitionSpec as P

EXACT = lax.Precision.HIGHEST
F32, BF16 = jnp.float32, jnp.bfloat16
RIM = 16


def dot(a, b, dims=((1,), (0,)), precision=None):
    return lax.dot_general(
        a, b, (dims, ((), ())), preferred_element_type=F32, precision=precision
    )


def shifted(x, taps_at, branch, length):
    start = RIM - taps_at if branch == 0 else taps_at
    return x[start : start + length]


def head_lanes(per_head_col, first, group, depth, length):
    lane = lax.broadcasted_iota(jnp.int32, (length, group * depth), 1)
    value = jnp.broadcast_to(per_head_col[:, first : first + 1], lane.shape)
    for extra in range(1, group):
        value = jnp.where(
            lane >= extra * depth,
            jnp.broadcast_to(per_head_col[:, first + extra : first + extra + 1], lane.shape),
            value,
        )
    return value


def local_kernel(
    depth, group, xf, xr, back, sizes, run, run_t, writes, reads, taps, gain,
    mixed, base, slopes, states, skip,
):
    length, width = back.shape
    row = lax.broadcasted_iota(jnp.int32, (length, length), 0)
    col = lax.broadcasted_iota(jnp.int32, (length, length), 1)
    scores = []
    for b in range(2):
        full = dot(reads[b], writes[b], ((1,), (1,)), EXACT)
        scores.append(jnp.where(row >= col if b == 0 else row <= col, full, 0.0))
    span = group * depth
    lane = lax.broadcasted_iota(jnp.int32, (length, span), 1)
    for q in range(width // span):
        cols = slice(q * span, (q + 1) * span)
        grad = back[:, cols]
        grad16 = grad.astype(BF16)
        total = None
        acts = None
        for b in range(2):
            x = (xf, xr)[b][:, cols].astype(F32)
            before = sum(
                taps[k : k + 1, cols] * shifted(x, k, b, length) for k in range(taps.shape[0])
            )
            sigma = jax.nn.sigmoid(before)
            act = before * sigma
            slope = sigma * (1.0 + before * (1.0 - sigma))
            size = head_lanes(sizes[b], q * group, group, depth, length)
            source = act * size
            source16 = source.astype(BF16)
            scan = adjoint = None
            for g in range(group):
                h = q * group + g
                spread = run[b, :, h : h + 1] - run_t[b, h : h + 1, :]
                decay = (jnp.exp(jnp.minimum(spread, 0.0)) * scores[b]).astype(BF16)
                one = dot(decay, source16)
                two = dot(decay, grad16, ((0,), (0,)))
                scan = one if g == 0 else jnp.where(lane >= g * depth, one, scan)
                adjoint = two if g == 0 else jnp.where(lane >= g * depth, two, adjoint)
            running = head_lanes(run[b], q * group, group, depth, length)
            end = running[length - 1 :] if b == 0 else running[:1]
            remain = jnp.exp(end - running)
            states[b, :, cols] = dot(
                writes[b].astype(BF16), (source * remain).astype(BF16), ((0,), (0,))
            ).astype(BF16)
            states[2 + b, :, cols] = dot(
                reads[b].astype(BF16), (grad * jnp.exp(running)).astype(BF16), ((0,), (0,))
            ).astype(BF16)
            base[b, :, cols] = (gain[:, cols] * grad + size * adjoint) * slope
            slopes[b, :, cols] = slope * size * remain
            total = scan if b == 0 else total + scan
            acts = act if b == 0 else acts + act
        mixed[:, cols] = total + gain[:, cols] * acts
        skip[:, cols] = jnp.sum(grad * acts, axis=0, keepdims=True)


def carry_kernel(
    depth, group, xf, xr, mixed_in, base, slopes, run, writes, reads, carried, taps,
    mixed, inner, edge, slope_edge, filt,
):
    length, width = mixed_in.shape
    span = group * depth
    taken = taps.shape[0]
    zeros = jnp.zeros((8, span), F32)
    for q in range(width // span):
        cols = slice(q * span, (q + 1) * span)
        total = mixed_in[:, cols]
        grads = [0.0] * taken
        for b in range(2):
            running = head_lanes(run[b], q * group, group, depth, length)
            total = total + jnp.exp(running) * dot(
                reads[b].astype(BF16), carried[b, :, cols].astype(BF16)
            )
            slope = base[b, :, cols] + slopes[b, :, cols] * dot(
                writes[b].astype(BF16), carried[2 + b, :, cols].astype(BF16)
            )
            x = (xf, xr)[b][:, cols].astype(F32)
            for k in range(taken):
                grads[k] = grads[k] + jnp.sum(
                    slope * shifted(x, k, b, length), axis=0, keepdims=True
                )
            if b == 0:
                longer = jnp.concatenate([slope, zeros], axis=0)
                parts = [longer[k : k + length] for k in range(taken)]
                slope_edge[b, :, cols] = slope[:8]
            else:
                longer = jnp.concatenate([zeros, slope], axis=0)
                parts = [longer[8 - k : 8 - k + length] for k in range(taken)]
                slope_edge[b, :, cols] = slope[length - 8 :]
            grad = sum(taps[k : k + 1, cols] * parts[k] for k in range(taken))
            inner[b * length : (b + 1) * length, cols] = grad.astype(BF16)
            edge[b, :, cols] = grad[length - 8 :] if b == 0 else grad[:8]
        mixed[:, cols] = total.astype(BF16)
        for k in range(taken):
            filt[k : k + 1, cols] = grads[k]


def three_parts(value):
    parts = []
    for _ in range(3):
        top = lax.reduce_precision(value, 8, 7)
        parts.append(top.astype(BF16))
        value = value - top
    rows = jnp.concatenate(parts, 0)
    return jnp.pad(rows, ((0, -rows.shape[0] % 16), (0, 0)))


def summed_whole(value, axis):
    count = lax.axis_size(axis)
    for b in range(count.bit_length() - 1):
        value = value + lax.ppermute(value, axis, [(i, i ^ (1 << b)) for i in range(count)])
    return value


def entering(ends, totals, axis):
    count, me = lax.axis_size(axis), lax.axis_index(axis)
    kinds, states, width = ends.shape
    rows = kinds * states
    group = ends.astype(F32)
    result = jnp.zeros_like(group)
    passed = jnp.zeros((kinds, width), F32)
    forward = jnp.array([True, False, False, True])
    for b in range(count.bit_length() - 1):
        bit = 1 << b
        packed = jnp.concatenate(
            [group.astype(BF16).reshape(rows, width), three_parts(totals)], 0
        )
        arrived = lax.ppermute(packed, axis, [(i, i ^ bit) for i in range(count)]).astype(F32)
        other = arrived[:rows].reshape(kinds, states, width)
        added = sum(arrived[rows + 2 * k : rows + 2 * k + 2] for k in range(3))
        source = (forward == ((me // bit) % 2 == 1))[:, None]
        theirs, ours = jnp.tile(added, (2, 1)), jnp.tile(totals, (2, 1))
        result = result + jnp.where(source, jnp.exp(passed), 0.0)[:, None] * other
        passed = passed + jnp.where(source, theirs, 0.0)
        group = (
            jnp.where(source, jnp.exp(ours), 1.0)[:, None] * other
            + jnp.where(source, 1.0, jnp.exp(theirs))[:, None] * group
        )
        totals = totals + added
    return result


def summed_rows(value, axis, beside):
    count, me = lax.axis_size(axis), lax.axis_index(axis)
    bits = [1 << b for b in range(count.bit_length() - 1)]
    orders = (bits, bits[:1] + bits[2:] + bits[1:2])
    half = value.shape[0] // 2
    parts = [value[:half], value[half:]]

    def swapped(part, bit):
        return lax.ppermute(part, axis, [(i, i ^ bit) for i in range(count)])

    for step in range(len(bits)):
        for p in range(2):
            bit = orders[p][step]
            upper = (me // bit) % 2
            rows = parts[p].shape[0] // 2
            keep = lax.dynamic_slice_in_dim(parts[p], upper * rows, rows, 0)
            send = lax.dynamic_slice_in_dim(parts[p], (1 - upper) * rows, rows, 0)
            parts[p] = (keep.astype(F32) + swapped(send, bit).astype(F32)).astype(BF16)
    parts, beside = lax.optimization_barrier((parts, beside))
    for step in reversed(range(len(bits))):
        for p in range(2):
            bit = orders[p][step]
            upper = (me // bit) % 2
            other = swapped(parts[p], bit)
            parts[p] = jnp.where(
                upper == 0,
                jnp.concatenate([parts[p], other], 0),
                jnp.concatenate([other, parts[p]], 0),
            )
    return jnp.concatenate(parts, 0), beside


def vmem_call(body, shapes, *operands):
    spec = pl.BlockSpec(memory_space=pltpu.VMEM)
    return pl.pallas_call(
        body,
        out_shape=[jax.ShapeDtypeStruct(*s) for s in shapes],
        in_specs=[spec] * len(operands),
        out_specs=[spec] * len(shapes),
        compiler_params=pltpu.CompilerParams(vmem_limit_bytes=48 * 1024 * 1024),
    )(*operands)


def per_device(
    hidden, channel_perm, input_weight, state_weight, step_weight, step_bias, decay_log,
    filter_taps, skip_gain, output_weight, cotangent,
):
    length = hidden.shape[0]
    taken, width = filter_taps.shape
    heads = step_weight.shape[1]
    depth = width // heads
    group = max(1, 128 // depth)
    states = state_weight.shape[1] // 2
    model = input_weight.shape[0]
    count, me = lax.axis_size("ctx"), lax.axis_index("ctx")
    pair = lax.axis_size("ch") == 2
    side = lax.axis_index("ch")
    up = [(i, i + 1) for i in range(count - 1)]
    down = [(i + 1, i) for i in range(count - 1)]
    swap = [(0, 1), (1, 0)]

    def gathered(part):
        if not pair:
            return lax.all_gather(part, "ch", axis=1, tiled=True)
        other = lax.ppermute(part, "ch", swap)
        return jnp.where(
            side == 0,
            jnp.concatenate([part, other], 1),
            jnp.concatenate([other, part], 1),
        )

    embed = gathered(hidden)
    upstream = gathered(cotangent)
    onehot = (
        lax.broadcasted_iota(jnp.int32, (model, model), 0) == channel_perm[None, :]
    ).astype(BF16)
    both = jnp.concatenate([embed, dot(embed, onehot).astype(BF16)], 0)
    inner = dot(both, input_weight).astype(BF16)
    small = dot(both, jnp.concatenate([state_weight, step_weight], 1)).reshape(2, length, -1)
    fwd_rim = lax.ppermute(inner[length - RIM : length], "ctx", up)
    rev_rim = lax.ppermute(inner[length : length + RIM], "ctx", down)
    writes = small[:, :, :states]
    reads = small[:, :, states : 2 * states]
    sizes = jax.nn.softplus(small[:, :, 2 * states :] + step_bias[None, None, :])
    decays = -jnp.exp(decay_log)[None, None, :] * sizes
    totals = jnp.repeat(jnp.sum(decays, axis=1), depth, axis=1)
    lower = jnp.tril(jnp.ones((length, length), F32))
    sums = jnp.stack([lower, lower.T])
    run = jnp.einsum("bts,bsh->bth", sums, decays, precision=EXACT)
    run_t = jnp.swapaxes(run, 1, 2)
    back = dot(upstream, output_weight, ((1,), (1,)))
    xf = jnp.concatenate([fwd_rim, inner[:length]], 0)
    xr = jnp.concatenate([inner[length:], rev_rim], 0)
    full = (length, width)
    mixed, base, slopes, ends, skip = vmem_call(
        functools.partial(local_kernel, depth, group),
        [
            (full, F32),
            ((2,) + full, F32),
            ((2,) + full, F32),
            ((4, states, width), BF16),
            ((1, width), F32),
        ],
        xf, xr, back, sizes, run, run_t, writes, reads, filter_taps, skip_gain[None, :],
    )
    carried = entering(ends, totals, "ctx")
    mixed16, partial_grad, edge, slope_edge, filt = vmem_call(
        functools.partial(carry_kernel, depth, group),
        [
            (full, BF16),
            ((2 * length, width), BF16),
            ((2, 8, width), F32),
            ((2, 8, width), F32),
            ((taken, width), F32),
        ],
        xf, xr, mixed, base, slopes, run, writes, reads, carried, filter_taps,
    )
    fwd_after = lax.ppermute(slope_edge[0], "ctx", down)
    rev_after = lax.ppermute(slope_edge[1], "ctx", up)
    if pair:
        half = output_weight.shape[1] // 2
        theirs = lax.dynamic_slice_in_dim(output_weight, (1 - side) * half, half, 1)
        mine = lax.dynamic_slice_in_dim(output_weight, side * half, half, 1)
        arrived = lax.ppermute(dot(mixed16, theirs).astype(BF16), "ch", swap)
        layer_out = (dot(mixed16, mine) + arrived.astype(F32)).astype(BF16)
    else:
        layer_out = lax.psum_scatter(
            dot(mixed16, output_weight), "ch", scatter_dimension=1, tiled=True
        ).astype(BF16)
    zeros = jnp.zeros((8, width), F32)
    ahead = jnp.concatenate([zeros, fwd_after], 0)
    behind = jnp.concatenate([rev_after, zeros], 0)
    fwd_edge = edge[0] + sum(filter_taps[k][None] * ahead[k : k + 8] for k in range(taken))
    rev_edge = edge[1] + sum(
        filter_taps[k][None] * behind[8 - k : 16 - k] for k in range(taken)
    )
    grad_inner = jnp.concatenate(
        [
            partial_grad[: length - 8],
            fwd_edge.astype(BF16),
            rev_edge.astype(BF16),
            partial_grad[length + 8 :],
        ],
        0,
    )
    weight_local = dot(both, grad_inner, ((0,), (0,))).astype(BF16)
    tiny = summed_whole(jnp.concatenate([filt, skip], 0), "ctx")
    weight_grad, (tiny, layer_out) = summed_rows(weight_local, "ctx", (tiny, layer_out))
    weight_grad = weight_grad.astype(F32)
    return (layer_out, weight_grad, tiny[:taken], tiny[taken])


def solution(mesh):
    placed = (
        P("ctx", "ch"), P(), P(None, "ch"), P(), P(None, "ch"), P("ch"), P("ch"),
        P(None, "ch"), P("ch"), P("ch", None), P("ctx", "ch"),
    )
    return jax.shard_map(
        per_device,
        mesh=mesh,
        in_specs=placed,
        out_specs=(P("ctx", "ch"), P(None, "ch"), P(None, "ch"), P("ch")),
        check_vma=False,
    )
```
